32 devices in a mesh: teacher: 4 (over y, core), seq: 8 (over z, x).
Axes of the slice: x: 2, y: 2, z: 4, core: 2. Of those that a mesh axis runs over, the one named last changes fastest.
Arguments:
- activations: bfloat16 [20, 512, 1536], P('teacher', 'seq'), may hold values from -150 to 150
- teacher_maps: bfloat16 [4, 20, 512, 1536], P('teacher', None, 'seq'), may hold values from -6 to 6
- projection: bfloat16 [4, 1536, 1536], P('teacher', 'seq'), may hold values from -0.4375 to 0.4375
- dilated_weight: bfloat16 [1536, 3, 768], P('seq'), may hold values from -0.09375 to 0.09375
- pointwise_weight: bfloat16 [768, 1536], P('seq'), may hold values from -0.21875 to 0.21875
Outputs:
- loss_mean: float32 [], replicated
- dilated_grad: float32 [1536, 3, 768], P('seq')
- pointwise_grad: float32 [768, 1536], P('seq')
The draws below stay inside these ranges and needn't reach their ends.
All inputs are finite; a program needn't handle non-finite values.
Results may differ from the reference program's by a relative error of at most 0.00081.
Values may be sent and summed in bfloat16 or wider, within the bound.
A program may use at most 128 MiB of HBM per device.

```python
import jax
import jax.numpy as jnp
from jax import lax

STUDENT_CHANNELS = 1536
CH = 768
CT = 1536
TAP_DILATION = 16
TEACHERS = 4
WINDOWS = 20
WINDOW_BINS = 512


def draw_activations(key, part):
    keyed = jax.random.fold_in(key, 17)
    key_base, key_rows, key_cols = jax.random.split(keyed, 3)
    full_shape = (WINDOWS, WINDOW_BINS, STUDENT_CHANNELS)
    baseline = jnp.clip(jax.random.normal(key_base, full_shape, jnp.float32), -6.0, 6.0)
    rise_factor = 3.0
    roughness = jnp.exp(jax.random.uniform(key_rows, (WINDOWS, WINDOW_BINS, 1), jnp.float32, 0.0, 2.302585))
    columns_scale = jnp.exp(jax.random.uniform(key_cols, (1, 1, STUDENT_CHANNELS), jnp.float32, 0.0, 2.302585))
    trend_rise = jnp.exp(jnp.log(rise_factor) * (1.0 - jnp.arange(WINDOW_BINS, dtype=jnp.float32) / WINDOW_BINS)).reshape(1, WINDOW_BINS, 1)
    return (0.05 * baseline * roughness * columns_scale * trend_rise).astype(jnp.bfloat16)


def raised(array, stream_key, source, target, shards_of, factor):
    owner, partner = [(jnp.arange(array.shape[axis_at]) // (array.shape[axis_at] // shards_of)).reshape([-1 if axis == axis_at else 1 for axis in range(array.ndim)]) for axis_at in (source, target)]
    chosen = jax.random.permutation(stream_key, shards_of)[partner]
    strong = (owner == chosen) | (owner == (partner + shards_of // 2) % shards_of)
    return jnp.where(strong, factor * array, array)


def steps_of(key, shape, shards, low, largest):
    level, own = 1.0, jax.random.fold_in(key, 6)
    for dim, parts in shards:
        heights = jnp.exp(jax.random.uniform(jax.random.fold_in(own, dim), (parts,), jnp.float32, low / len(shards), largest / len(shards)))
        level = level * jnp.repeat(heights, shape[dim] // parts).reshape([-1 if axis == dim else 1 for axis in range(len(shape))])
    return level


def scatter_about(rng, shape, width, limit, pieces=(), held_as=jnp.bfloat16):
    result = jax.random.normal(rng, shape, jnp.float32) * width
    if len(pieces) > 0:
        result = steps_of(rng, shape, pieces, -0.22, 0.18) * result
    return jnp.clip(result, min=-limit, max=limit).astype(held_as)


def heavy_noise(key, extent, width, most, pieces, heavy, kind=jnp.bfloat16):
    array = width * jax.random.normal(key, extent, jnp.float32)
    if pieces:
        array = array * steps_of(key, extent, pieces, -0.22, 0.18)
    return jnp.clip(raised(array, jax.random.fold_in(key, 3), *heavy), -most, most).astype(kind)


def setup_inputs(seed: int = 0) -> dict:
    arg_keys = jax.random.split(jax.random.key(seed), 6)
    return {
        "activations": draw_activations(jax.random.fold_in(arg_keys[5], 71), 0),
        "teacher_maps": scatter_about(arg_keys[1], (TEACHERS, WINDOWS, WINDOW_BINS, CT), 1.0, 6.0, ((0, 4), (2, 8))),
        "projection": heavy_noise(arg_keys[2], (TEACHERS, CT, STUDENT_CHANNELS), (CT // 4) ** -0.5, 0.4375, ((0, 4), (1, 8)), (1, 2, 8, 2.0)),
        "dilated_weight": scatter_about(arg_keys[3], (STUDENT_CHANNELS, 3, CH), (3 * STUDENT_CHANNELS) ** -0.5, 0.09375, ((0, 8),)),
        "pointwise_weight": scatter_about(arg_keys[4], (CH, STUDENT_CHANNELS), CH ** -0.5, 0.21875, ((0, 8),)),
    }


slope_const = 0.7978845608
cubic_const = 0.044715

def gelu_tanh(value):
    inside = slope_const * (value + cubic_const * value * value * value)
    return 0.5 * value * (1.0 + jnp.tanh(inside))

def gelu_slope(value):
    inside = slope_const * (value + cubic_const * value * value * value)
    tangent = jnp.tanh(inside)
    return 0.5 * (1.0 + tangent) + 0.5 * value * (1.0 - tangent * tangent) * slope_const * (1.0 + 3.0 * cubic_const * value * value)

def reference(activations, teacher_maps, projection, dilated_weight, pointwise_weight):
    count_of_rows = WINDOWS * WINDOW_BINS
    target = jnp.zeros((count_of_rows, STUDENT_CHANNELS), jnp.float32)
    for teacher_id in range(TEACHERS):
        maps_flat = teacher_maps[teacher_id].reshape(count_of_rows, CT)
        rounded = lax.optimization_barrier(jnp.dot(maps_flat, projection[teacher_id], preferred_element_type=jnp.float32).astype(jnp.bfloat16))
        target = target + rounded.astype(jnp.float32)
    target = target / TEACHERS
    inputs_f = activations.reshape(count_of_rows, STUDENT_CHANNELS).astype(jnp.float32)
    channel_mean = lax.optimization_barrier(jnp.sum(inputs_f, axis=0)) / count_of_rows
    channel_var = lax.optimization_barrier(jnp.sum(inputs_f * inputs_f, axis=0)) / count_of_rows - channel_mean * channel_mean
    normed = (inputs_f - channel_mean) * lax.rsqrt(channel_var + 1e-05)
    hidden_state = gelu_tanh(normed).astype(jnp.bfloat16).reshape(WINDOWS, WINDOW_BINS, STUDENT_CHANNELS)
    padded_input = jnp.pad(hidden_state, ((0, 0), (TAP_DILATION, TAP_DILATION), (0, 0)))
    tap_weights = [padded_input[:, offset_index * TAP_DILATION:offset_index * TAP_DILATION + WINDOW_BINS].reshape(count_of_rows, STUDENT_CHANNELS) for offset_index in range(3)]
    preact = jnp.zeros((count_of_rows, CH), jnp.float32)
    for offset_index in range(3):
        preact = preact + jnp.dot(tap_weights[offset_index], dilated_weight[:, offset_index, :], preferred_element_type=jnp.float32)
    activated = gelu_tanh(preact).astype(jnp.bfloat16)
    student = inputs_f + jnp.dot(activated, pointwise_weight, preferred_element_type=jnp.float32)
    misfit = student - target
    loss_mean = 0.5 * jnp.sum(misfit * misfit) / (STUDENT_CHANNELS * count_of_rows)
    out_grad = (misfit / STUDENT_CHANNELS).astype(jnp.bfloat16)
    pointwise_grad = lax.dot_general(activated, out_grad, (((0,), (0,)), ((), ())), preferred_element_type=jnp.float32)
    back_grad = lax.dot_general(out_grad, pointwise_weight, (((1,), (1,)), ((), ())), preferred_element_type=jnp.float32)
    preact_grad = (back_grad * gelu_slope(preact)).astype(jnp.bfloat16)
    dilated_grad = jnp.stack([lax.dot_general(tap_weights[offset_index], preact_grad, (((0,), (0,)), ((), ())), preferred_element_type=jnp.float32) for offset_index in range(3)], axis=1)
    return (loss_mean, dilated_grad, pointwise_grad)
```

```python
import functools

import jax
import jax.numpy as jnp
from jax import lax
from jax.experimental import pallas as pl
from jax.experimental.pallas import tpu as pltpu
from jax.sharding import PartitionSpec as P

TAP_DILATION = 16

slope_const = 0.7978845608
cubic_const = 0.044715

MESH = pl.DeviceIdType.MESH
HBM = pl.BlockSpec(memory_space=pl.ANY)
VMEM = pl.BlockSpec(memory_space=pltpu.VMEM)


class Link:
    def __init__(self, send, recv):
        self.send, self.recv, self.used, self.started = send, recv, 0, []

    def take(self, count):
        first = self.used
        self.used += count
        return first

    def copy(self, src, dst, slot, device):
        return pltpu.make_async_remote_copy(
            src_ref=src,
            dst_ref=dst,
            send_sem=self.send.at[slot],
            recv_sem=self.recv.at[slot],
            device_id=device,
            device_id_type=MESH,
        )

    def start(self, src, dst, slot, device):
        put = self.copy(src, dst, slot, device)
        put.start()
        self.started.append(put)

    def arrived(self, dst, slot, device):
        self.copy(dst, dst, slot, device).wait_recv()

    def drain(self):
        for put in self.started:
            put.wait_send()


class Place:
    def __init__(self, groups, ranks):
        self.groups, self.ranks = groups, ranks
        self.t, self.s = lax.axis_index("teacher"), lax.axis_index("seq")
        self.core = self.t % 2
        self.bit = self.s % 2
        self.col = self.s // 2
        self.cols = ranks // 2
        self.sibling = {"teacher": self.t + 1 - 2 * self.core}
        self.across = {"teacher": (self.t + 2) % groups}
        self.partner = {"seq": self.s + 1 - 2 * self.bit}

    def later(self, step):
        return (self.s + step) % self.ranks

    def earlier(self, step):
        return (self.s + self.ranks - step) % self.ranks

    def barrier(self, seq=True, teacher=True):
        sem = pltpu.get_barrier_semaphore()
        count = 0
        if seq:
            for step in range(1, self.ranks):
                pl.semaphore_signal(
                    sem, inc=1, device_id={"seq": self.later(step)}, device_id_type=MESH
                )
                count += 1
        if teacher:
            for step in range(1, self.groups):
                pl.semaphore_signal(
                    sem,
                    inc=1,
                    device_id={"teacher": (self.t + step) % self.groups},
                    device_id_type=MESH,
                )
                count += 1
        pl.semaphore_wait(sem, count)


class Gather:
    def __init__(self, place, link, source, piece, sibling_piece=None):
        self.place, self.link, self.source = place, link, source
        self.piece, self.sibling_piece = piece, sibling_piece
        self.down = link.take(place.cols)
        self.over = link.take(place.cols)
        self.side = link.take(place.ranks) if sibling_piece else None

    def shard(self, step, bit):
        place = self.place
        return ((place.col + place.cols - step) % place.cols) * 2 + bit

    def start(self):
        place, link = self.place, self.link
        for step in range(1, place.cols):
            peer = ((place.col + step) % place.cols) * 2 + place.bit
            link.start(self.source, self.piece(place.s), self.down + step, {"seq": peer})
        link.start(self.source, self.piece(place.s), self.over, place.partner)

    def forward(self):
        place, link = self.place, self.link
        for step in range(1, place.cols):
            ref = self.piece(self.shard(step, place.bit))
            link.arrived(ref, self.down + step, place.partner)
            link.start(ref, ref, self.over + step, place.partner)
            if self.side is not None:
                link.start(ref, ref, self.side + step, place.sibling)

    def collect(self):
        place, link = self.place, self.link
        for step in range(place.cols):
            ref = self.piece(self.shard(step, 1 - place.bit))
            link.arrived(ref, self.over + step, place.partner)
            if self.side is not None:
                link.start(ref, ref, self.side + place.cols + step, place.sibling)

    def finish(self):
        place, link = self.place, self.link
        if self.side is None:
            return
        for step in range(1, place.cols):
            ref = self.sibling_piece(self.shard(step, place.bit))
            link.arrived(ref, self.side + step, place.sibling)
        for step in range(place.cols):
            ref = self.sibling_piece(self.shard(step, 1 - place.bit))
            link.arrived(ref, self.side + place.cols + step, place.sibling)


def total_of(place, link, own, stage_t, stage_s):
    to_t, to_s = link.take(place.groups), link.take(place.ranks)

    def first():
        stage_t[place.t] = own[...]
        for step in range(1, place.groups):
            link.start(
                own,
                stage_t.at[place.t],
                to_t + step,
                {"teacher": (place.t + step) % place.groups},
            )

    def second():
        for step in range(1, place.groups):
            giver = (place.t + place.groups - step) % place.groups
            link.arrived(stage_t.at[giver], to_t + step, place.sibling)
        summed = stage_t[0]
        for group in range(1, place.groups):
            summed = summed + stage_t[group]
        stage_s[place.s] = summed
        for step in range(1, place.ranks):
            link.start(
                stage_s.at[place.s],
                stage_s.at[place.s],
                to_s + step,
                {"seq": place.later(step)},
            )

    def third():
        for step in range(1, place.ranks):
            link.arrived(stage_s.at[place.earlier(step)], to_s + step, place.partner)
        summed = stage_s[0]
        for rank in range(1, place.ranks):
            summed = summed + stage_s[rank]
        return summed

    return first, second, third


def projection_kernel(groups, ranks, proj, stats, full, totals, stage_t, stage_s, send, recv, local):
    place, link = Place(groups, ranks), Link(send, recv)
    place.barrier()
    keep = pltpu.make_async_copy(proj, full.at[place.s], local.at[0])
    keep.start()
    first, second, third = total_of(place, link, stats, stage_t, stage_s)
    gather = Gather(place, link, proj, lambda j: full.at[j])
    first()
    gather.start()
    second()
    totals[...] = third()
    gather.forward()
    gather.collect()
    keep.wait()
    link.drain()


def forward_kernel(
    groups, ranks, terms, dilated, pointwise, panels, hidden,
    terms_all, dilated_all, pointwise_all, panels_all, halo, send, recv, local,
):
    place, link = Place(groups, ranks), Link(send, recv)
    half_d, half_p = dilated.shape[2] // 2, pointwise.shape[1] // 2
    bins = hidden.shape[1]
    place.barrier()

    def columns(core, half):
        return pl.ds(pl.multiple_of(core * half, half), half)

    mine_d, mine_p = columns(place.core, half_d), columns(place.core, half_p)
    other_d, other_p = columns(1 - place.core, half_d), columns(1 - place.core, half_p)
    to_t, to_s, edges = link.take(groups), link.take(ranks), link.take(2)
    after, before = {"seq": place.later(1)}, {"seq": place.earlier(1)}
    link.start(hidden.at[:, pl.ds(bins - TAP_DILATION, TAP_DILATION)], halo.at[0], edges, after)
    link.start(hidden.at[:, pl.ds(0, TAP_DILATION)], halo.at[1], edges + 1, before)
    for step in range(1, groups):
        taker = (place.t + step) % groups
        link.start(terms.at[taker], terms_all.at[place.t], to_t + step, {"teacher": taker})
    gather_d = Gather(
        place,
        link,
        dilated.at[:, :, mine_d],
        lambda j: dilated_all.at[:, j, :, mine_d],
        lambda j: dilated_all.at[:, j, :, other_d],
    )
    gather_p = Gather(
        place,
        link,
        pointwise.at[:, mine_p],
        lambda j: pointwise_all.at[j, :, mine_p],
        lambda j: pointwise_all.at[j, :, other_p],
    )
    gather_d.start()
    gather_p.start()
    for step in range(1, ranks):
        taker = place.later(step)
        link.start(panels.at[taker], panels_all.at[place.s], to_s + step, {"seq": taker})
    keeps = [
        pltpu.make_async_copy(terms.at[place.t], terms_all.at[place.t], local.at[0]),
        pltpu.make_async_copy(dilated, dilated_all.at[:, place.s], local.at[1]),
        pltpu.make_async_copy(pointwise, pointwise_all.at[place.s], local.at[2]),
        pltpu.make_async_copy(panels.at[place.s], panels_all.at[place.s], local.at[3]),
    ]
    for keep in keeps:
        keep.start()
    gather_d.forward()
    gather_p.forward()
    gather_d.collect()
    gather_p.collect()
    gather_d.finish()
    gather_p.finish()
    link.arrived(halo.at[0], edges, after)
    link.arrived(halo.at[1], edges + 1, before)
    for step in range(1, groups):
        giver = (place.t + groups - step) % groups
        link.arrived(terms_all.at[giver], to_t + step, place.sibling)
    for step in range(1, ranks):
        link.arrived(panels_all.at[place.earlier(step)], to_s + step, place.partner)
    for keep in keeps:
        keep.wait()
    link.drain()


def backward_kernel(
    groups, ranks, slopes, partial, loss,
    slopes_all, shares, loss_total,
    from_core, from_chip, pieces, stage_t, stage_s, send, recv, local,
):
    place, link = Place(groups, ranks), Link(send, recv)
    width = partial.shape[1] // groups
    rows = partial.shape[0] // ranks
    place.barrier()
    keep = pltpu.make_async_copy(slopes, slopes_all.at[place.s], local.at[0])
    keep.start()
    to_core, to_chip, to_s, to_t = (link.take(count) for count in (1, 1, ranks, groups))
    high = place.t // 2

    def columns(index, size):
        return pl.ds(pl.multiple_of(index * size, size), size)

    link.start(partial.at[:, columns(1 - place.core, 2 * width)], from_core, to_core, place.sibling)
    first, second, third = total_of(place, link, loss, stage_t, stage_s)
    first()
    gather = Gather(place, link, slopes, lambda j: slopes_all.at[j])
    gather.start()
    link.arrived(from_core, to_core, place.sibling)
    mine = columns(place.core, 2 * width)

    @pl.loop(0, ranks)
    def _(rank):
        span = pl.ds(pl.multiple_of(rank * rows, rows), rows)
        from_core[span] = from_core[span] + partial[span, mine]

    link.start(from_core.at[:, columns(1 - high, width)], from_chip, to_chip, place.across)
    second()
    loss_total[...] = third()
    link.arrived(from_chip, to_chip, place.across)
    kept = columns(high, width)

    @pl.loop(0, ranks)
    def _(rank):
        span = pl.ds(pl.multiple_of(rank * rows, rows), rows)
        from_chip[span] = from_chip[span] + from_core[span, kept]

    for step in range(1, ranks):
        taker = place.later(step)
        span = pl.ds(pl.multiple_of(taker * rows, rows), rows)
        link.start(from_chip.at[span], pieces.at[place.s], to_s + step, {"seq": taker})
    gather.forward()
    own = pl.ds(pl.multiple_of(place.s * rows, rows), rows)
    pieces[place.s] = from_chip[own]
    for step in range(1, ranks):
        link.arrived(pieces.at[place.earlier(step)], to_s + step, place.partner)
    summed = pieces[0]
    for rank in range(1, ranks):
        summed = summed + pieces[rank]
    slot = place.core * 2 + high
    shares[slot] = summed
    for step in range(1, groups):
        link.start(
            shares.at[slot],
            shares.at[slot],
            to_t + step,
            {"teacher": (place.t + step) % groups},
        )
    gather.collect()
    for step in range(1, groups):
        giver = (place.t + groups - step) % groups
        link.arrived(shares.at[(giver % 2) * 2 + giver // 2], to_t + step, place.sibling)
    keep.wait()
    link.drain()


def share_kernel(groups, ranks, partial, out, from_core, from_chip, send, recv):
    place, link = Place(groups, ranks), Link(send, recv)
    taps, rows, width = partial.shape
    half = width // 2
    place.barrier(seq=False)
    a, b, c = link.take(taps), link.take(taps), link.take(taps)

    def columns(core):
        return pl.ds(pl.multiple_of(core * half, half), half)

    mine, other = columns(place.core), columns(1 - place.core)
    for tap in range(taps):
        link.start(partial.at[tap, :, other], from_core.at[tap], a + tap, place.sibling)
    for tap in range(taps):
        link.arrived(from_core.at[tap], a + tap, place.sibling)
        from_core[tap] = from_core[tap] + partial[tap, :, mine]
        link.start(from_core.at[tap], from_chip.at[tap], b + tap, place.across)
    for tap in range(taps):
        link.arrived(from_chip.at[tap], b + tap, place.across)
        out[tap, :, mine] = from_chip[tap] + from_core[tap]
        link.start(out.at[tap, :, mine], out.at[tap, :, mine], c + tap, place.sibling)
    for tap in range(taps):
        link.arrived(out.at[tap, :, other], c + tap, place.sibling)
    link.drain()


def exchange(kernel, number, groups, ranks, args, specs, outs, out_specs, scratch, copies, locals_):
    sems = [pltpu.SemaphoreType.DMA((copies,)), pltpu.SemaphoreType.DMA((copies,))]
    if locals_:
        sems.append(pltpu.SemaphoreType.DMA((locals_,)))
    return pl.pallas_call(
        functools.partial(kernel, groups, ranks),
        out_shape=[jax.ShapeDtypeStruct(shape, kind) for shape, kind in outs],
        in_specs=specs,
        out_specs=out_specs,
        scratch_shapes=[pltpu.VMEM(shape, kind) for shape, kind in scratch] + sems,
        compiler_params=pltpu.CompilerParams(
            collective_id=number, has_side_effects=True, vmem_limit_bytes=40 * 1024 * 1024
        ),
    )(*args)


def gelu_tanh(value):
    inside = slope_const * (value + cubic_const * value * value * value)
    return 0.5 * value * (1.0 + jnp.tanh(inside))


def gelu_slope(value):
    inside = slope_const * (value + cubic_const * value * value * value)
    tangent = jnp.tanh(inside)
    return 0.5 * (1.0 + tangent) + 0.5 * value * (1.0 - tangent * tangent) * slope_const * (
        1.0 + 3.0 * cubic_const * value * value
    )


def column_product(left, right):
    return lax.dot_general(
        left, right, (((0,), (0,)), ((), ())), preferred_element_type=jnp.float32
    )


def shards(activations, teacher_maps, projection, dilated_weight, pointwise_weight):
    groups = lax.axis_size("teacher")
    ranks = lax.axis_size("seq")
    f32, bf16 = jnp.float32, jnp.bfloat16
    win_grp, bins, channels = activations.shape
    branch = dilated_weight.shape[2]
    panel = dilated_weight.shape[0]
    features = projection.shape[1]
    rows = win_grp * bins
    total_rows = rows * groups * ranks
    rank = lax.axis_index("seq")

    inputs_f = activations.reshape(rows, channels).astype(f32)
    stats = jnp.concatenate(
        [
            jnp.sum(inputs_f, axis=0, keepdims=True),
            jnp.sum(inputs_f * inputs_f, axis=0, keepdims=True),
            jnp.zeros((6, channels), f32),
        ]
    )
    proj_full, totals = exchange(
        projection_kernel, 0, groups, ranks,
        (projection[0], stats), [HBM, VMEM],
        [((ranks, features, channels), bf16), ((8, channels), f32)], [HBM, VMEM],
        [((groups, 8, channels), f32), ((ranks, 8, channels), f32)],
        2 * ranks + groups, 1,
    )
    channel_mean = totals[0] / total_rows
    channel_var = totals[1] / total_rows - channel_mean * channel_mean
    normed = (inputs_f - channel_mean) * lax.rsqrt(channel_var + 1e-05)
    hidden = gelu_tanh(normed).astype(bf16)
    hidden_3d = hidden.reshape(win_grp, bins, channels)
    panels = jnp.stack([hidden[:, j * panel : (j + 1) * panel] for j in range(ranks)])
    terms = jnp.dot(
        teacher_maps[0].reshape(groups * rows, -1),
        proj_full.reshape(ranks * features, channels),
        preferred_element_type=f32,
    ).astype(bf16)

    terms_all, dilated_all, pointwise_all, panels_all, halo = exchange(
        forward_kernel, 1, groups, ranks,
        (
            terms.reshape(groups, rows, channels),
            dilated_weight.transpose(1, 0, 2),
            pointwise_weight,
            panels,
            hidden_3d,
        ),
        [HBM] * 5,
        [
            ((groups, rows, channels), bf16),
            ((3, ranks, panel, branch), bf16),
            ((ranks,) + pointwise_weight.shape, bf16),
            ((ranks, rows, panel), bf16),
            ((2, win_grp, TAP_DILATION, channels), bf16),
        ],
        [HBM] * 5,
        [],
        5 * ranks + groups + 2, 4,
    )
    target = terms_all[0].astype(f32)
    for group in range(1, groups):
        target = target + terms_all[group].astype(f32)
    target = target / groups

    low = jnp.where(rank > 0, halo[0], jnp.zeros_like(halo[0]))
    high = jnp.where(rank < ranks - 1, halo[1], jnp.zeros_like(halo[1]))
    padded = jnp.concatenate([low, hidden_3d, high], axis=1)
    preact = jnp.zeros((rows, branch), f32)
    for tap in range(3):
        shifted = padded[:, tap * TAP_DILATION : tap * TAP_DILATION + bins].reshape(rows, channels)
        preact = preact + jnp.dot(
            shifted, dilated_all[tap].reshape(channels, branch), preferred_element_type=f32
        )
    activated = gelu_tanh(preact).astype(bf16)
    pointwise_full = pointwise_all.reshape(branch, channels)
    student = inputs_f + jnp.dot(activated, pointwise_full, preferred_element_type=f32)
    misfit = student - target
    squared = jnp.sum(misfit * misfit)
    out_grad = (misfit / channels).astype(bf16)
    back_grad = lax.dot_general(
        out_grad, pointwise_full, (((1,), (1,)), ((), ())), preferred_element_type=f32
    )
    preact_grad = (back_grad * gelu_slope(preact)).astype(bf16)
    pointwise_part = column_product(activated, out_grad)

    slopes_all, shares, loss_total = exchange(
        backward_kernel, 2, groups, ranks,
        (preact_grad, pointwise_part, jnp.full((8, 128), squared, f32)),
        [HBM, VMEM, VMEM],
        [
            ((ranks, rows, branch), bf16),
            ((groups, branch // ranks, channels // groups), f32),
            ((8, 128), f32),
        ],
        [HBM, VMEM, VMEM],
        [
            ((branch, channels // 2), f32),
            ((branch, channels // groups), f32),
            ((ranks, branch // ranks, channels // groups), f32),
            ((groups, 8, 128), f32),
            ((ranks, 8, 128), f32),
        ],
        3 * ranks + 2 * groups + 2, 1,
    )
    loss_mean = 0.5 * loss_total[0, 0] / (channels * total_rows)
    pointwise_grad = shares.transpose(1, 0, 2).reshape(branch // ranks, channels)

    def windows(blocks):
        return (
            blocks.reshape(ranks, win_grp, bins, -1)
            .transpose(1, 0, 2, 3)
            .reshape(win_grp, ranks * bins, -1)
        )

    hidden_w = jnp.pad(windows(panels_all), ((0, 0), (TAP_DILATION, TAP_DILATION), (0, 0)))
    slopes_w = windows(slopes_all).reshape(win_grp * ranks * bins, branch)
    partial = jnp.stack(
        [
            column_product(
                hidden_w[:, tap * TAP_DILATION : tap * TAP_DILATION + ranks * bins].reshape(
                    win_grp * ranks * bins, panel
                ),
                slopes_w,
            )
            for tap in range(3)
        ]
    )
    (dilated_grad,) = exchange(
        share_kernel, 3, groups, ranks,
        (partial,), [VMEM],
        [((3, panel, branch), f32)], [VMEM],
        [((3, panel, branch // 2), f32), ((3, panel, branch // 2), f32)],
        9, 0,
    )
    return (loss_mean, dilated_grad.transpose(1, 0, 2), pointwise_grad)


def solution(mesh):
    in_specs = (
        P("teacher", "seq", None),
        P("teacher", None, "seq", None),
        P("teacher", "seq", None),
        P("seq", None, None),
        P("seq", None),
    )
    out_specs = (P(), P("seq", None, None), P("seq", None))
    return jax.shard_map(shards, mesh=mesh, in_specs=in_specs, out_specs=out_specs, check_vma=False)
```

```python
import functools

import jax
import jax.numpy as jnp
from jax import lax
from jax.experimental import pallas as pl
from jax.experimental.pallas import tpu as pltpu
from jax.sharding import PartitionSpec as P

TAP_DILATION = 16

slope_const = 0.7978845608
cubic_const = 0.044715

MESH = pl.DeviceIdType.MESH
HBM = pl.BlockSpec(memory_space=pl.ANY)
VMEM = pl.BlockSpec(memory_space=pltpu.VMEM)


class Link:
    def __init__(self, send, recv):
        self.send, self.recv, self.used, self.started = send, recv, 0, []

    def take(self, count):
        first = self.used
        self.used += count
        return first

    def copy(self, src, dst, slot, device):
        return pltpu.make_async_remote_copy(
            src_ref=src,
            dst_ref=dst,
            send_sem=self.send.at[slot],
            recv_sem=self.recv.at[slot],
            device_id=device,
            device_id_type=MESH,
        )

    def start(self, src, dst, slot, device):
        put = self.copy(src, dst, slot, device)
        put.start()
        self.started.append(put)

    def arrived(self, dst, slot, device):
        self.copy(dst, dst, slot, device).wait_recv()

    def drain(self):
        for put in self.started:
            put.wait_send()


class Place:
    def __init__(self, groups, ranks):
        self.groups, self.ranks = groups, ranks
        self.t, self.s = lax.axis_index("teacher"), lax.axis_index("seq")
        self.core = self.t % 2
        self.bit = self.s % 2
        self.col = self.s // 2
        self.cols = ranks // 2
        self.sibling = {"teacher": self.t + 1 - 2 * self.core}
        self.across = {"teacher": (self.t + 2) % groups}
        self.partner = {"seq": self.s + 1 - 2 * self.bit}

    def later(self, step):
        return (self.s + step) % self.ranks

    def earlier(self, step):
        return (self.s + self.ranks - step) % self.ranks

    def barrier(self, seq=True, teacher=True):
        sem = pltpu.get_barrier_semaphore()
        count = 0
        if seq:
            for step in range(1, self.ranks):
                pl.semaphore_signal(
                    sem, inc=1, device_id={"seq": self.later(step)}, device_id_type=MESH
                )
                count += 1
        if teacher:
            for step in range(1, self.groups):
                pl.semaphore_signal(
                    sem,
                    inc=1,
                    device_id={"teacher": (self.t + step) % self.groups},
                    device_id_type=MESH,
                )
                count += 1
        pl.semaphore_wait(sem, count)


class Gather:
    def __init__(self, place, link, source, piece, chunks, spread=None):
        self.place, self.link, self.source, self.piece = place, link, source, piece
        self.chunks, self.spread = chunks, spread
        self.down = [link.take(place.cols) for _ in range(chunks)]
        self.over = [link.take(place.cols) for _ in range(chunks)]

    def shard(self, index):
        place = self.place
        bit = place.bit if index < place.cols else 1 - place.bit
        return ((place.col + place.cols - index % place.cols) % place.cols) * 2 + bit

    def start(self):
        place, link = self.place, self.link
        for chunk in range(self.chunks):
            source, target = self.source(chunk), self.piece(place.s, chunk)
            link.start(source, target, self.over[chunk], place.partner)
            for step in range(1, place.cols):
                peer = ((place.col + step) % place.cols) * 2 + place.bit
                link.start(source, target, self.down[chunk] + step, {"seq": peer})

    def forward(self, chunk):
        place, link = self.place, self.link
        for step in range(1, place.cols):
            shard = self.shard(step)
            ref = self.piece(shard, chunk)
            link.arrived(ref, self.down[chunk] + step, place.partner)
            link.start(ref, ref, self.over[chunk] + step, place.partner)
            if self.spread is not None:
                self.spread(shard, chunk, step)

    def collect(self, chunk):
        place, link = self.place, self.link
        for step in range(place.cols):
            shard = self.shard(place.cols + step)
            link.arrived(self.piece(shard, chunk), self.over[chunk] + step, place.partner)
            if self.spread is not None:
                self.spread(shard, chunk, place.cols + step)


def total_of(place, link, own, stage_t, stage_s):
    to_t, to_s = link.take(place.groups), link.take(place.ranks)

    def first():
        stage_t[place.t] = own[...]
        for step in range(1, place.groups):
            link.start(
                own,
                stage_t.at[place.t],
                to_t + step,
                {"teacher": (place.t + step) % place.groups},
            )

    def second():
        for step in range(1, place.groups):
            giver = (place.t + place.groups - step) % place.groups
            link.arrived(stage_t.at[giver], to_t + step, place.sibling)
        summed = stage_t[0]
        for group in range(1, place.groups):
            summed = summed + stage_t[group]
        stage_s[place.s] = summed
        for step in range(1, place.ranks):
            link.start(
                stage_s.at[place.s],
                stage_s.at[place.s],
                to_s + step,
                {"seq": place.later(step)},
            )

    def third():
        for step in range(1, place.ranks):
            link.arrived(stage_s.at[place.earlier(step)], to_s + step, place.partner)
        summed = stage_s[0]
        for rank in range(1, place.ranks):
            summed = summed + stage_s[rank]
        return summed

    return first, second, third


def columns(index, size):
    return pl.ds(pl.multiple_of(index * size, size), size)


def projection_kernel(
    groups, ranks, proj, dilated, stats, full, dilated_all, totals,
    stage_t, stage_s, send, recv, local,
):
    place, link = Place(groups, ranks), Link(send, recv)
    chunks = 4
    width = proj.shape[1] // chunks
    half = dilated.shape[2] // 2
    high = place.t // 2
    mine, other = columns(place.core, half), columns(1 - place.core, half)
    taps = (2 * high, 1, 2 - 2 * high)
    side, across = [link.take(ranks) for _ in taps], link.take(ranks)

    def to_sibling(shard, chunk, index):
        ref = dilated_all.at[taps[chunk], shard, :, mine]
        link.start(ref, ref, side[chunk] + index, place.sibling)

    def spread(shard, chunk, index):
        if chunk == 0:
            ref = dilated_all.at[taps[0], shard, :, mine]
            link.start(ref, ref, across + index, place.across)
        to_sibling(shard, chunk, index)

    place.barrier()
    keeps = [
        pltpu.make_async_copy(proj, full.at[place.s], local.at[0]),
        pltpu.make_async_copy(dilated, dilated_all.at[:, place.s], local.at[1]),
    ]
    for keep in keeps:
        keep.start()
    first, second, third = total_of(place, link, stats, stage_t, stage_s)
    gather = Gather(
        place,
        link,
        lambda q: proj.at[:, pl.ds(q * width, width)],
        lambda j, q: full.at[j, :, pl.ds(q * width, width)],
        chunks,
    )
    gather_d = Gather(
        place,
        link,
        lambda q: dilated.at[taps[q], :, mine],
        lambda j, q: dilated_all.at[taps[q], j, :, mine],
        2,
        spread,
    )
    first()
    gather_d.start()
    gather.start()
    second()
    for chunk in range(2):
        gather_d.forward(chunk)
        gather.forward(chunk)
    for chunk in range(2):
        gather_d.collect(chunk)
        gather.forward(2 + chunk)
    for index in range(1, ranks):
        shard = gather_d.shard(index)
        link.arrived(dilated_all.at[taps[2], shard, :, mine], across + index, place.across)
        to_sibling(shard, 2, index)
    totals[...] = third()
    for chunk in range(chunks):
        gather.collect(chunk)
    for index in range(1, ranks):
        for chunk in range(3):
            ref = dilated_all.at[taps[chunk], gather_d.shard(index), :, other]
            link.arrived(ref, side[chunk] + index, place.sibling)
    for keep in keeps:
        keep.wait()
    link.drain()


def forward_kernel(
    groups, ranks, terms, pointwise, panels, hidden,
    terms_all, pointwise_all, panels_all, halo, send, recv, local,
):
    place, link = Place(groups, ranks), Link(send, recv)
    half = pointwise.shape[1] // 2
    bins = hidden.shape[1]
    place.barrier()
    mine, other = columns(place.core, half), columns(1 - place.core, half)
    to_t, to_s, edges, side = (link.take(count) for count in (groups, ranks, 2, ranks))
    after, before = {"seq": place.later(1)}, {"seq": place.earlier(1)}

    def spread(shard, chunk, index):
        ref = pointwise_all.at[shard, :, mine]
        link.start(ref, ref, side + index, place.sibling)

    for step in range(1, groups):
        taker = (place.t + step) % groups
        link.start(terms.at[taker], terms_all.at[place.t], to_t + step, {"teacher": taker})
    gather = Gather(
        place,
        link,
        lambda q: pointwise.at[:, mine],
        lambda j, q: pointwise_all.at[j, :, mine],
        1,
        spread,
    )
    gather.start()
    link.start(hidden.at[:, pl.ds(bins - TAP_DILATION, TAP_DILATION)], halo.at[0], edges, after)
    link.start(hidden.at[:, pl.ds(0, TAP_DILATION)], halo.at[1], edges + 1, before)
    for step in range(1, ranks):
        taker = place.later(step)
        link.start(panels.at[taker], panels_all.at[place.s], to_s + step, {"seq": taker})
    keeps = [
        pltpu.make_async_copy(terms.at[place.t], terms_all.at[place.t], local.at[0]),
        pltpu.make_async_copy(pointwise, pointwise_all.at[place.s], local.at[1]),
        pltpu.make_async_copy(panels.at[place.s], panels_all.at[place.s], local.at[2]),
    ]
    for keep in keeps:
        keep.start()
    gather.forward(0)
    gather.collect(0)
    for index in range(1, ranks):
        ref = pointwise_all.at[gather.shard(index), :, other]
        link.arrived(ref, side + index, place.sibling)
    link.arrived(halo.at[0], edges, after)
    link.arrived(halo.at[1], edges + 1, before)
    for step in range(1, groups):
        giver = (place.t + groups - step) % groups
        link.arrived(terms_all.at[giver], to_t + step, place.sibling)
    for step in range(1, ranks):
        link.arrived(panels_all.at[place.earlier(step)], to_s + step, place.partner)
    for keep in keeps:
        keep.wait()
    link.drain()


def backward_kernel(
    groups, ranks, slopes, partial, loss,
    slopes_all, shares, loss_total,
    from_core, from_chip, pieces, stage_t, stage_s, send, recv, local,
):
    place, link = Place(groups, ranks), Link(send, recv)
    width = partial.shape[1] // groups
    rows = partial.shape[0] // ranks
    place.barrier()
    keep = pltpu.make_async_copy(slopes, slopes_all.at[place.s], local.at[0])
    keep.start()
    to_core, to_chip, to_s, to_t = (link.take(count) for count in (1, 1, ranks, groups))
    high = place.t // 2

    link.start(partial.at[:, columns(1 - place.core, 2 * width)], from_core, to_core, place.sibling)
    first, second, third = total_of(place, link, loss, stage_t, stage_s)
    first()
    chunks = 3
    part = slopes.shape[1] // chunks
    gather = Gather(
        place,
        link,
        lambda q: slopes.at[:, pl.ds(q * part, part)],
        lambda j, q: slopes_all.at[j, :, pl.ds(q * part, part)],
        chunks,
    )
    gather.start()
    link.arrived(from_core, to_core, place.sibling)
    mine = columns(place.core, 2 * width)

    @pl.loop(0, ranks)
    def _(rank):
        span = pl.ds(pl.multiple_of(rank * rows, rows), rows)
        from_core[span] = from_core[span] + partial[span, mine]

    link.start(from_core.at[:, columns(1 - high, width)], from_chip, to_chip, place.across)
    gather.forward(0)
    second()
    gather.forward(1)
    link.arrived(from_chip, to_chip, place.across)
    kept = columns(high, width)

    @pl.loop(0, ranks)
    def _(rank):
        span = pl.ds(pl.multiple_of(rank * rows, rows), rows)
        from_chip[span] = from_chip[span] + from_core[span, kept]

    for step in range(1, ranks):
        taker = place.later(step)
        span = pl.ds(pl.multiple_of(taker * rows, rows), rows)
        link.start(from_chip.at[span], pieces.at[place.s], to_s + step, {"seq": taker})
    gather.forward(2)
    gather.collect(0)
    own = pl.ds(pl.multiple_of(place.s * rows, rows), rows)
    pieces[place.s] = from_chip[own]
    for step in range(1, ranks):
        link.arrived(pieces.at[place.earlier(step)], to_s + step, place.partner)
    summed = pieces[0]
    for rank in range(1, ranks):
        summed = summed + pieces[rank]
    slot = place.core * 2 + high
    shares[slot] = summed
    for step in range(1, groups):
        link.start(
            shares.at[slot],
            shares.at[slot],
            to_t + step,
            {"teacher": (place.t + step) % groups},
        )
    gather.collect(1)
    gather.collect(2)
    loss_total[...] = third()
    for step in range(1, groups):
        giver = (place.t + groups - step) % groups
        link.arrived(shares.at[(giver % 2) * 2 + giver // 2], to_t + step, place.sibling)
    keep.wait()
    link.drain()


def share_kernel(groups, ranks, partial, out, from_core, from_chip, send, recv):
    place, link = Place(groups, ranks), Link(send, recv)
    taps, rows, width = partial.shape
    half = width // 2
    place.barrier(seq=False)
    a, b, c = link.take(taps), link.take(taps), link.take(taps)

    def columns(core):
        return pl.ds(pl.multiple_of(core * half, half), half)

    mine, other = columns(place.core), columns(1 - place.core)
    for tap in range(taps):
        link.start(partial.at[tap, :, other], from_core.at[tap], a + tap, place.sibling)
    for tap in range(taps):
        link.arrived(from_core.at[tap], a + tap, place.sibling)
        from_core[tap] = from_core[tap] + partial[tap, :, mine]
        link.start(from_core.at[tap], from_chip.at[tap], b + tap, place.across)
    for tap in range(taps):
        link.arrived(from_chip.at[tap], b + tap, place.across)
        out[tap, :, mine] = from_chip[tap] + from_core[tap]
        link.start(out.at[tap, :, mine], out.at[tap, :, mine], c + tap, place.sibling)
    for tap in range(taps):
        link.arrived(out.at[tap, :, other], c + tap, place.sibling)
    link.drain()


def exchange(kernel, number, groups, ranks, args, specs, outs, out_specs, scratch, copies, locals_):
    sems = [pltpu.SemaphoreType.DMA((copies,)), pltpu.SemaphoreType.DMA((copies,))]
    if locals_:
        sems.append(pltpu.SemaphoreType.DMA((locals_,)))
    return pl.pallas_call(
        functools.partial(kernel, groups, ranks),
        out_shape=[jax.ShapeDtypeStruct(shape, kind) for shape, kind in outs],
        in_specs=specs,
        out_specs=out_specs,
        scratch_shapes=[pltpu.VMEM(shape, kind) for shape, kind in scratch] + sems,
        compiler_params=pltpu.CompilerParams(
            collective_id=number, has_side_effects=True, vmem_limit_bytes=40 * 1024 * 1024
        ),
    )(*args)


def gelu_tanh(value):
    inside = slope_const * (value + cubic_const * value * value * value)
    return 0.5 * value * (1.0 + jnp.tanh(inside))


def gelu_slope(value):
    inside = slope_const * (value + cubic_const * value * value * value)
    tangent = jnp.tanh(inside)
    return 0.5 * (1.0 + tangent) + 0.5 * value * (1.0 - tangent * tangent) * slope_const * (
        1.0 + 3.0 * cubic_const * value * value
    )


def column_product(left, right):
    return lax.dot_general(
        left, right, (((0,), (0,)), ((), ())), preferred_element_type=jnp.float32
    )


def shards(activations, teacher_maps, projection, dilated_weight, pointwise_weight):
    groups = lax.axis_size("teacher")
    ranks = lax.axis_size("seq")
    f32, bf16 = jnp.float32, jnp.bfloat16
    win_grp, bins, channels = activations.shape
    branch = dilated_weight.shape[2]
    panel = dilated_weight.shape[0]
    features = projection.shape[1]
    rows = win_grp * bins
    total_rows = rows * groups * ranks
    rank = lax.axis_index("seq")

    inputs_f = activations.reshape(rows, channels).astype(f32)
    stats = jnp.concatenate(
        [
            jnp.sum(inputs_f, axis=0, keepdims=True),
            jnp.sum(inputs_f * inputs_f, axis=0, keepdims=True),
            jnp.zeros((6, channels), f32),
        ]
    )
    proj_full, dilated_all, totals = exchange(
        projection_kernel, 0, groups, ranks,
        (projection[0], dilated_weight.transpose(1, 0, 2), stats), [HBM, HBM, VMEM],
        [
            ((ranks, features, channels), bf16),
            ((3, ranks, panel, branch), bf16),
            ((8, channels), f32),
        ],
        [HBM, HBM, VMEM],
        [((groups, 8, channels), f32), ((ranks, 8, channels), f32)],
        11 * ranks + groups, 2,
    )
    channel_mean = totals[0] / total_rows
    channel_var = totals[1] / total_rows - channel_mean * channel_mean
    normed = (inputs_f - channel_mean) * lax.rsqrt(channel_var + 1e-05)
    hidden = gelu_tanh(normed).astype(bf16)
    hidden_3d = hidden.reshape(win_grp, bins, channels)
    panels = jnp.stack([hidden[:, j * panel : (j + 1) * panel] for j in range(ranks)])
    terms = jnp.dot(
        teacher_maps[0].reshape(groups * rows, -1),
        proj_full.reshape(ranks * features, channels),
        preferred_element_type=f32,
    ).astype(bf16)

    terms_all, pointwise_all, panels_all, halo = exchange(
        forward_kernel, 1, groups, ranks,
        (
            terms.reshape(groups, rows, channels),
            pointwise_weight,
            panels,
            hidden_3d,
        ),
        [HBM] * 4,
        [
            ((groups, rows, channels), bf16),
            ((ranks,) + pointwise_weight.shape, bf16),
            ((ranks, rows, panel), bf16),
            ((2, win_grp, TAP_DILATION, channels), bf16),
        ],
        [HBM] * 4,
        [],
        3 * ranks + groups + 2, 3,
    )
    target = terms_all[0].astype(f32)
    for group in range(1, groups):
        target = target + terms_all[group].astype(f32)
    target = target / groups

    low = jnp.where(rank > 0, halo[0], jnp.zeros_like(halo[0]))
    high = jnp.where(rank < ranks - 1, halo[1], jnp.zeros_like(halo[1]))
    padded = jnp.concatenate([low, hidden_3d, high], axis=1)
    shifted = jnp.concatenate(
        [padded[:, tap * TAP_DILATION : tap * TAP_DILATION + bins] for tap in range(3)], axis=2
    )
    preact = jnp.dot(
        shifted.reshape(rows, 3 * channels),
        dilated_all.reshape(3 * channels, branch),
        preferred_element_type=f32,
    )
    activated = gelu_tanh(preact).astype(bf16)
    pointwise_full = pointwise_all.reshape(branch, channels)
    student = inputs_f + jnp.dot(activated, pointwise_full, preferred_element_type=f32)
    misfit = student - target
    squared = jnp.sum(misfit * misfit)
    out_grad = (misfit / channels).astype(bf16)
    back_grad = lax.dot_general(
        out_grad, pointwise_full, (((1,), (1,)), ((), ())), preferred_element_type=f32
    )
    preact_grad = (back_grad * gelu_slope(preact)).astype(bf16)
    pointwise_part = column_product(activated, out_grad)

    slopes_all, shares, loss_total = exchange(
        backward_kernel, 2, groups, ranks,
        (preact_grad, pointwise_part, jnp.full((8, 128), squared, f32)),
        [HBM, VMEM, VMEM],
        [
            ((ranks, rows, branch), bf16),
            ((groups, branch // ranks, channels // groups), f32),
            ((8, 128), f32),
        ],
        [HBM, VMEM, VMEM],
        [
            ((branch, channels // 2), f32),
            ((branch, channels // groups), f32),
            ((ranks, branch // ranks, channels // groups), f32),
            ((groups, 8, 128), f32),
            ((ranks, 8, 128), f32),
        ],
        5 * ranks + 2 * groups + 2, 1,
    )
    loss_mean = 0.5 * loss_total[0, 0] / (channels * total_rows)
    pointwise_grad = shares.transpose(1, 0, 2).reshape(branch // ranks, channels)

    def windows(blocks):
        return (
            blocks.reshape(ranks, win_grp, bins, -1)
            .transpose(1, 0, 2, 3)
            .reshape(win_grp, ranks * bins, -1)
        )

    hidden_w = jnp.pad(windows(panels_all), ((0, 0), (TAP_DILATION, TAP_DILATION), (0, 0)))
    slopes_w = windows(slopes_all).reshape(win_grp * ranks * bins, branch)
    partial = jnp.stack(
        [
            column_product(
                hidden_w[:, tap * TAP_DILATION : tap * TAP_DILATION + ranks * bins].reshape(
                    win_grp * ranks * bins, panel
                ),
                slopes_w,
            )
            for tap in range(3)
        ]
    )
    (dilated_grad,) = exchange(
        share_kernel, 3, groups, ranks,
        (partial,), [VMEM],
        [((3, panel, branch), f32)], [VMEM],
        [((3, panel, branch // 2), f32), ((3, panel, branch // 2), f32)],
        9, 0,
    )
    return (loss_mean, dilated_grad.transpose(1, 0, 2), pointwise_grad)


def solution(mesh):
    in_specs = (
        P("teacher", "seq", None),
        P("teacher", None, "seq", None),
        P("teacher", "seq", None),
        P("seq", None, None),
        P("seq", None),
    )
    out_specs = (P(), P("seq", None, None), P("seq", None))
    return jax.shard_map(shards, mesh=mesh, in_specs=in_specs, out_specs=out_specs, check_vma=False)
```

```python
import functools

import jax
import jax.numpy as jnp
from jax import lax
from jax.experimental import pallas as pl
from jax.experimental.pallas import tpu as pltpu
from jax.sharding import PartitionSpec as P

TAP_DILATION = 16

slope_const = 0.7978845608
cubic_const = 0.044715

MESH = pl.DeviceIdType.MESH
HBM = pl.BlockSpec(memory_space=pl.ANY)
VMEM = pl.BlockSpec(memory_space=pltpu.VMEM)


class Link:
    def __init__(self, send, recv):
        self.send, self.recv, self.used, self.started = send, recv, 0, []

    def take(self, count):
        first = self.used
        self.used += count
        return first

    def copy(self, src, dst, slot, device):
        return pltpu.make_async_remote_copy(
            src_ref=src,
            dst_ref=dst,
            send_sem=self.send.at[slot],
            recv_sem=self.recv.at[slot],
            device_id=device,
            device_id_type=MESH,
        )

    def start(self, src, dst, slot, device):
        put = self.copy(src, dst, slot, device)
        put.start()
        self.started.append(put)

    def arrived(self, dst, slot, device):
        self.copy(dst, dst, slot, device).wait_recv()

    def drain(self):
        for put in self.started:
            put.wait_send()


class Place:
    def __init__(self, groups, ranks):
        self.groups, self.ranks = groups, ranks
        self.t, self.s = lax.axis_index("teacher"), lax.axis_index("seq")
        self.core = self.t % 2
        self.bit = self.s % 2
        self.col = self.s // 2
        self.cols = ranks // 2
        self.sibling = {"teacher": self.t + 1 - 2 * self.core}
        self.across = {"teacher": (self.t + 2) % groups}
        self.partner = {"seq": self.s + 1 - 2 * self.bit}

    def later(self, step):
        return (self.s + step) % self.ranks

    def earlier(self, step):
        return (self.s + self.ranks - step) % self.ranks

    def barrier(self, seq=True, teacher=True):
        sem = pltpu.get_barrier_semaphore()
        count = 0
        if seq:
            for step in range(1, self.ranks):
                pl.semaphore_signal(
                    sem, inc=1, device_id={"seq": self.later(step)}, device_id_type=MESH
                )
                count += 1
        if teacher:
            for step in range(1, self.groups):
                pl.semaphore_signal(
                    sem,
                    inc=1,
                    device_id={"teacher": (self.t + step) % self.groups},
                    device_id_type=MESH,
                )
                count += 1
        pl.semaphore_wait(sem, count)


class Gather:
    def __init__(self, place, link, source, piece, chunks, spread=None):
        self.place, self.link, self.source, self.piece = place, link, source, piece
        self.chunks, self.spread = chunks, spread
        self.down = [link.take(place.cols) for _ in range(chunks)]
        self.over = [link.take(place.cols) for _ in range(chunks)]

    def shard(self, index):
        place = self.place
        bit = place.bit if index < place.cols else 1 - place.bit
        return ((place.col + place.cols - index % place.cols) % place.cols) * 2 + bit

    def start(self):
        place, link = self.place, self.link
        for chunk in range(self.chunks):
            source, target = self.source(chunk), self.piece(place.s, chunk)
            link.start(source, target, self.over[chunk], place.partner)
            for step in range(1, place.cols):
                peer = ((place.col + step) % place.cols) * 2 + place.bit
                link.start(source, target, self.down[chunk] + step, {"seq": peer})

    def forward(self, chunk):
        place, link = self.place, self.link
        for step in range(1, place.cols):
            shard = self.shard(step)
            ref = self.piece(shard, chunk)
            link.arrived(ref, self.down[chunk] + step, place.partner)
            link.start(ref, ref, self.over[chunk] + step, place.partner)
            if self.spread is not None:
                self.spread(shard, chunk, step)

    def collect(self, chunk):
        place, link = self.place, self.link
        for step in range(place.cols):
            shard = self.shard(place.cols + step)
            link.arrived(self.piece(shard, chunk), self.over[chunk] + step, place.partner)
            if self.spread is not None:
                self.spread(shard, chunk, place.cols + step)


def total_of(place, link, own, stage_t, stage_s):
    to_t, to_s = link.take(place.groups), link.take(place.ranks)

    def first():
        stage_t[place.t] = own[...]
        for step in range(1, place.groups):
            link.start(
                own,
                stage_t.at[place.t],
                to_t + step,
                {"teacher": (place.t + step) % place.groups},
            )

    def second():
        for step in range(1, place.groups):
            giver = (place.t + place.groups - step) % place.groups
            link.arrived(stage_t.at[giver], to_t + step, place.sibling)
        summed = stage_t[0]
        for group in range(1, place.groups):
            summed = summed + stage_t[group]
        stage_s[place.s] = summed
        for step in range(1, place.ranks):
            link.start(
                stage_s.at[place.s],
                stage_s.at[place.s],
                to_s + step,
                {"seq": place.later(step)},
            )

    def third():
        for step in range(1, place.ranks):
            link.arrived(stage_s.at[place.earlier(step)], to_s + step, place.partner)
        summed = stage_s[0]
        for rank in range(1, place.ranks):
            summed = summed + stage_s[rank]
        return summed

    return first, second, third


def columns(index, size):
    return pl.ds(pl.multiple_of(index * size, size), size)


def projection_kernel(
    groups, ranks, proj, dilated, stats, full, dilated_all, totals,
    stage_t, stage_s, send, recv, local,
):
    place, link = Place(groups, ranks), Link(send, recv)
    chunks = 6
    width = proj.shape[1] // chunks
    half = dilated.shape[2] // 2
    high = place.t // 2
    mine, other = columns(place.core, half), columns(1 - place.core, half)
    taps = (2 * high, 1, 2 - 2 * high)
    side, across = [link.take(ranks) for _ in taps], link.take(ranks)

    def to_sibling(shard, chunk, index):
        ref = dilated_all.at[taps[chunk], shard, :, mine]
        link.start(ref, ref, side[chunk] + index, place.sibling)

    def spread(shard, chunk, index):
        if chunk == 0:
            ref = dilated_all.at[taps[0], shard, :, mine]
            link.start(ref, ref, across + index, place.across)
        to_sibling(shard, chunk, index)

    place.barrier()
    keeps = [
        pltpu.make_async_copy(proj, full.at[place.s], local.at[0]),
        pltpu.make_async_copy(dilated, dilated_all.at[:, place.s], local.at[1]),
    ]
    for keep in keeps:
        keep.start()
    first, second, third = total_of(place, link, stats, stage_t, stage_s)
    gather = Gather(
        place,
        link,
        lambda q: proj.at[:, pl.ds(q * width, width)],
        lambda j, q: full.at[j, :, pl.ds(q * width, width)],
        chunks,
    )
    gather_d = Gather(
        place,
        link,
        lambda q: dilated.at[taps[q], :, mine],
        lambda j, q: dilated_all.at[taps[q], j, :, mine],
        2,
        spread,
    )
    first()
    gather_d.start()
    gather.start()
    second()
    for chunk in range(2):
        gather_d.forward(chunk)
        gather.forward(chunk)
    for chunk in range(2):
        gather_d.collect(chunk)
        gather.forward(2 + 2 * chunk)
        gather.forward(3 + 2 * chunk)
    for index in range(1, ranks):
        shard = gather_d.shard(index)
        link.arrived(dilated_all.at[taps[2], shard, :, mine], across + index, place.across)
        to_sibling(shard, 2, index)
    totals[...] = third()
    for chunk in range(chunks):
        gather.collect(chunk)
    for index in range(1, ranks):
        for chunk in range(3):
            ref = dilated_all.at[taps[chunk], gather_d.shard(index), :, other]
            link.arrived(ref, side[chunk] + index, place.sibling)
    for keep in keeps:
        keep.wait()
    link.drain()


def forward_kernel(
    groups, ranks, terms, pointwise, panels, hidden,
    terms_all, pointwise_all, panels_all, halo, send, recv, local,
):
    place, link = Place(groups, ranks), Link(send, recv)
    chunks = 2
    part = pointwise.shape[1] // (2 * chunks)
    bins = hidden.shape[1]
    place.barrier()
    to_t, to_s, edges = (link.take(count) for count in (groups, ranks, 2))
    side = [link.take(ranks) for _ in range(chunks)]
    after, before = {"seq": place.later(1)}, {"seq": place.earlier(1)}

    def part_of(core, chunk):
        return columns(core * chunks + chunk, part)

    def spread(shard, chunk, index):
        ref = pointwise_all.at[shard, :, part_of(place.core, chunk)]
        link.start(ref, ref, side[chunk] + index, place.sibling)

    for step in range(1, groups):
        taker = (place.t + step) % groups
        link.start(terms.at[taker], terms_all.at[place.t], to_t + step, {"teacher": taker})
    gather = Gather(
        place,
        link,
        lambda q: pointwise.at[:, part_of(place.core, q)],
        lambda j, q: pointwise_all.at[j, :, part_of(place.core, q)],
        chunks,
        spread,
    )
    gather.start()
    link.start(hidden.at[:, pl.ds(bins - TAP_DILATION, TAP_DILATION)], halo.at[0], edges, after)
    link.start(hidden.at[:, pl.ds(0, TAP_DILATION)], halo.at[1], edges + 1, before)
    for step in range(1, ranks):
        taker = place.later(step)
        link.start(panels.at[taker], panels_all.at[place.s], to_s + step, {"seq": taker})
    keeps = [
        pltpu.make_async_copy(terms.at[place.t], terms_all.at[place.t], local.at[0]),
        pltpu.make_async_copy(pointwise, pointwise_all.at[place.s], local.at[1]),
        pltpu.make_async_copy(panels.at[place.s], panels_all.at[place.s], local.at[2]),
    ]
    for keep in keeps:
        keep.start()
    for chunk in range(chunks):
        gather.forward(chunk)
    for chunk in range(chunks):
        gather.collect(chunk)
    for index in range(1, ranks):
        for chunk in range(chunks):
            ref = pointwise_all.at[gather.shard(index), :, part_of(1 - place.core, chunk)]
            link.arrived(ref, side[chunk] + index, place.sibling)
    link.arrived(halo.at[0], edges, after)
    link.arrived(halo.at[1], edges + 1, before)
    for step in range(1, groups):
        giver = (place.t + groups - step) % groups
        link.arrived(terms_all.at[giver], to_t + step, place.sibling)
    for step in range(1, ranks):
        link.arrived(panels_all.at[place.earlier(step)], to_s + step, place.partner)
    for keep in keeps:
        keep.wait()
    link.drain()


def backward_kernel(
    groups, ranks, slopes, partial, loss,
    slopes_all, from_chip, loss_total,
    from_core, stage_t, stage_s, send, recv, local,
):
    place, link = Place(groups, ranks), Link(send, recv)
    width = partial.shape[1] // groups
    rows = partial.shape[0] // ranks
    place.barrier()
    keep = pltpu.make_async_copy(slopes, slopes_all.at[place.s], local.at[0])
    keep.start()
    to_core, to_chip = link.take(1), link.take(1)
    high = place.t // 2

    link.start(partial.at[:, columns(1 - place.core, 2 * width)], from_core, to_core, place.sibling)
    first, second, third = total_of(place, link, loss, stage_t, stage_s)
    first()
    chunks = 3
    part = slopes.shape[1] // chunks
    gather = Gather(
        place,
        link,
        lambda q: slopes.at[:, pl.ds(q * part, part)],
        lambda j, q: slopes_all.at[j, :, pl.ds(q * part, part)],
        chunks,
    )
    gather.start()
    link.arrived(from_core, to_core, place.sibling)
    mine = columns(place.core, 2 * width)

    @pl.loop(0, ranks)
    def _(rank):
        span = pl.ds(pl.multiple_of(rank * rows, rows), rows)
        from_core[span] = from_core[span] + partial[span, mine]

    link.start(from_core.at[:, columns(1 - high, width)], from_chip, to_chip, place.across)
    gather.forward(0)
    second()
    gather.forward(1)
    link.arrived(from_chip, to_chip, place.across)
    kept = columns(high, width)

    @pl.loop(0, ranks)
    def _(rank):
        span = pl.ds(pl.multiple_of(rank * rows, rows), rows)
        from_chip[span] = from_chip[span] + from_core[span, kept]

    gather.forward(2)
    for chunk in range(chunks):
        gather.collect(chunk)
    loss_total[...] = third()
    keep.wait()
    link.drain()


def share_kernel(
    groups, ranks, partial, block, out, shares, from_core, from_chip, pieces, send, recv
):
    place, link = Place(groups, ranks), Link(send, recv)
    taps, depth, branch = partial.shape
    half, tall = branch // 2, depth // 2
    rows, width = block.shape[0] // ranks, block.shape[1]
    parts = [(tap, pl.ds(low, tall)) for tap in range(taps) for low in (0, tall)]
    a, b, c = (link.take(len(parts)) for _ in range(3))
    to_s, to_t = link.take(ranks), link.take(groups)
    mine, other = columns(place.core, half), columns(1 - place.core, half)
    place.barrier()
    for at, (tap, span) in enumerate(parts):
        link.start(
            partial.at[tap, span, other], from_core.at[tap, span], a + at, place.sibling
        )
    for step in range(1, ranks):
        taker = place.later(step)
        span = pl.ds(pl.multiple_of(taker * rows, rows), rows)
        link.start(block.at[span], pieces.at[place.s], to_s + step, {"seq": taker})
    for at, (tap, span) in enumerate(parts):
        link.arrived(from_core.at[tap, span], a + at, place.sibling)
        from_core[tap, span] = from_core[tap, span] + partial[tap, span, mine]
        link.start(from_core.at[tap, span], from_chip.at[tap, span], b + at, place.across)
    pieces[place.s] = block[pl.ds(pl.multiple_of(place.s * rows, rows), rows)]

    def add_chip(at):
        tap, span = parts[at]
        link.arrived(from_chip.at[tap, span], b + at, place.across)
        out[tap, span, mine] = from_chip[tap, span] + from_core[tap, span]
        link.start(out.at[tap, span, mine], out.at[tap, span, mine], c + at, place.sibling)

    for at in range(len(parts) - 1):
        add_chip(at)
    for step in range(1, ranks):
        link.arrived(pieces.at[place.earlier(step)], to_s + step, place.partner)
    summed = pieces[0]
    for rank in range(1, ranks):
        summed = summed + pieces[rank]
    kept = columns(place.core * 2 + place.t // 2, width)
    shares[:, kept] = summed
    for step in range(1, groups):
        link.start(
            shares.at[:, kept],
            shares.at[:, kept],
            to_t + step,
            {"teacher": (place.t + step) % groups},
        )
    add_chip(len(parts) - 1)
    for at, (tap, span) in enumerate(parts):
        link.arrived(out.at[tap, span, other], c + at, place.sibling)
    for step in range(1, groups):
        giver = (place.t + groups - step) % groups
        ref = shares.at[:, columns((giver % 2) * 2 + giver // 2, width)]
        link.arrived(ref, to_t + step, place.sibling)
    link.drain()


def exchange(kernel, number, groups, ranks, args, specs, outs, out_specs, scratch, copies, locals_):
    sems = [pltpu.SemaphoreType.DMA((copies,)), pltpu.SemaphoreType.DMA((copies,))]
    if locals_:
        sems.append(pltpu.SemaphoreType.DMA((locals_,)))
    return pl.pallas_call(
        functools.partial(kernel, groups, ranks),
        out_shape=[jax.ShapeDtypeStruct(shape, kind) for shape, kind in outs],
        in_specs=specs,
        out_specs=out_specs,
        scratch_shapes=[pltpu.VMEM(shape, kind) for shape, kind in scratch] + sems,
        compiler_params=pltpu.CompilerParams(
            collective_id=number, has_side_effects=True, vmem_limit_bytes=40 * 1024 * 1024
        ),
    )(*args)


def gelu_tanh(value):
    inside = slope_const * (value + cubic_const * value * value * value)
    return 0.5 * value * (1.0 + jnp.tanh(inside))


def gelu_slope(value):
    inside = slope_const * (value + cubic_const * value * value * value)
    tangent = jnp.tanh(inside)
    return 0.5 * (1.0 + tangent) + 0.5 * value * (1.0 - tangent * tangent) * slope_const * (
        1.0 + 3.0 * cubic_const * value * value
    )


def column_product(left, right):
    return lax.dot_general(
        left, right, (((0,), (0,)), ((), ())), preferred_element_type=jnp.float32
    )


def shards(activations, teacher_maps, projection, dilated_weight, pointwise_weight):
    groups = lax.axis_size("teacher")
    ranks = lax.axis_size("seq")
    f32, bf16 = jnp.float32, jnp.bfloat16
    win_grp, bins, channels = activations.shape
    branch = dilated_weight.shape[2]
    panel = dilated_weight.shape[0]
    features = projection.shape[1]
    rows = win_grp * bins
    total_rows = rows * groups * ranks
    rank = lax.axis_index("seq")

    inputs_f = activations.reshape(rows, channels).astype(f32)
    stats = jnp.concatenate(
        [
            jnp.sum(inputs_f, axis=0, keepdims=True),
            jnp.sum(inputs_f * inputs_f, axis=0, keepdims=True),
            jnp.zeros((6, channels), f32),
        ]
    )
    proj_full, dilated_all, totals = exchange(
        projection_kernel, 0, groups, ranks,
        (projection[0], dilated_weight.transpose(1, 0, 2), stats), [HBM, HBM, VMEM],
        [
            ((ranks, features, channels), bf16),
            ((3, ranks, panel, branch), bf16),
            ((8, channels), f32),
        ],
        [HBM, HBM, VMEM],
        [((groups, 8, channels), f32), ((ranks, 8, channels), f32)],
        13 * ranks + groups, 2,
    )
    channel_mean = totals[0] / total_rows
    channel_var = totals[1] / total_rows - channel_mean * channel_mean
    normed = (inputs_f - channel_mean) * lax.rsqrt(channel_var + 1e-05)
    hidden = gelu_tanh(normed).astype(bf16)
    hidden_3d = hidden.reshape(win_grp, bins, channels)
    panels = jnp.stack([hidden[:, j * panel : (j + 1) * panel] for j in range(ranks)])
    terms = jnp.dot(
        teacher_maps[0].reshape(groups * rows, -1),
        proj_full.reshape(ranks * features, channels),
        preferred_element_type=f32,
    ).astype(bf16)

    terms_all, pointwise_all, panels_all, halo = exchange(
        forward_kernel, 1, groups, ranks,
        (
            terms.reshape(groups, rows, channels),
            pointwise_weight,
            panels,
            hidden_3d,
        ),
        [HBM] * 4,
        [
            ((groups, rows, channels), bf16),
            ((ranks,) + pointwise_weight.shape, bf16),
            ((ranks, rows, panel), bf16),
            ((2, win_grp, TAP_DILATION, channels), bf16),
        ],
        [HBM] * 4,
        [],
        5 * ranks + groups + 2, 3,
    )
    target = terms_all[0].astype(f32)
    for group in range(1, groups):
        target = target + terms_all[group].astype(f32)
    target = target / groups

    low = jnp.where(rank > 0, halo[0], jnp.zeros_like(halo[0]))
    high = jnp.where(rank < ranks - 1, halo[1], jnp.zeros_like(halo[1]))
    padded = jnp.concatenate([low, hidden_3d, high], axis=1)
    shifted = jnp.concatenate(
        [padded[:, tap * TAP_DILATION : tap * TAP_DILATION + bins] for tap in range(3)], axis=2
    )
    preact = jnp.dot(
        shifted.reshape(rows, 3 * channels),
        dilated_all.reshape(3 * channels, branch),
        preferred_element_type=f32,
    )
    activated = gelu_tanh(preact).astype(bf16)
    pointwise_full = pointwise_all.reshape(branch, channels)
    student = inputs_f + jnp.dot(activated, pointwise_full, preferred_element_type=f32)
    misfit = student - target
    squared = jnp.sum(misfit * misfit)
    out_grad = (misfit / channels).astype(bf16)
    back_grad = lax.dot_general(
        out_grad, pointwise_full, (((1,), (1,)), ((), ())), preferred_element_type=f32
    )
    preact_grad = (back_grad * gelu_slope(preact)).astype(bf16)
    pointwise_part = column_product(activated, out_grad)

    slopes_all, block, loss_total = exchange(
        backward_kernel, 2, groups, ranks,
        (preact_grad, pointwise_part, jnp.full((8, 128), squared, f32)),
        [HBM, VMEM, VMEM],
        [
            ((ranks, rows, branch), bf16),
            ((branch, channels // groups), f32),
            ((8, 128), f32),
        ],
        [HBM, VMEM, VMEM],
        [
            ((branch, channels // 2), f32),
            ((groups, 8, 128), f32),
            ((ranks, 8, 128), f32),
        ],
        4 * ranks + groups + 2, 1,
    )
    loss_mean = 0.5 * loss_total[0, 0] / (channels * total_rows)

    def windows(blocks):
        return (
            blocks.reshape(ranks, win_grp, bins, -1)
            .transpose(1, 0, 2, 3)
            .reshape(win_grp, ranks * bins, -1)
        )

    hidden_w = jnp.pad(windows(panels_all), ((0, 0), (TAP_DILATION, TAP_DILATION), (0, 0)))
    slopes_w = windows(slopes_all).reshape(win_grp * ranks * bins, branch)
    partial = jnp.stack(
        [
            column_product(
                hidden_w[:, tap * TAP_DILATION : tap * TAP_DILATION + ranks * bins].reshape(
                    win_grp * ranks * bins, panel
                ),
                slopes_w,
            )
            for tap in range(3)
        ]
    )
    dilated_grad, pointwise_grad = exchange(
        share_kernel, 3, groups, ranks,
        (partial, block), [VMEM, VMEM],
        [((3, panel, branch), f32), ((branch // ranks, channels), f32)], [VMEM, VMEM],
        [
            ((3, panel, branch // 2), f32),
            ((3, panel, branch // 2), f32),
            ((ranks, branch // ranks, channels // groups), f32),
        ],
        18 + ranks + groups, 0,
    )
    return (loss_mean, dilated_grad.transpose(1, 0, 2), pointwise_grad)


def solution(mesh):
    in_specs = (
        P("teacher", "seq", None),
        P("teacher", None, "seq", None),
        P("teacher", "seq", None),
        P("seq", None, None),
        P("seq", None),
    )
    out_specs = (P(), P("seq", None, None), P("seq", None))
    return jax.shard_map(shards, mesh=mesh, in_specs=in_specs, out_specs=out_specs, check_vma=False)
```

```python
import functools

import jax
import jax.numpy as jnp
from jax import lax
from jax.experimental import pallas as pl
from jax.experimental.pallas import tpu as pltpu
from jax.sharding import PartitionSpec as P

TAP_DILATION = 16

slope_const = 0.7978845608
cubic_const = 0.044715

MESH = pl.DeviceIdType.MESH
HBM = pl.BlockSpec(memory_space=pl.ANY)
VMEM = pl.BlockSpec(memory_space=pltpu.VMEM)


class Link:
    def __init__(self, send, recv):
        self.send, self.recv, self.used, self.started = send, recv, 0, []

    def take(self, count):
        first = self.used
        self.used += count
        return first

    def copy(self, src, dst, slot, device):
        return pltpu.make_async_remote_copy(
            src_ref=src,
            dst_ref=dst,
            send_sem=self.send.at[slot],
            recv_sem=self.recv.at[slot],
            device_id=device,
            device_id_type=MESH,
        )

    def start(self, src, dst, slot, device):
        put = self.copy(src, dst, slot, device)
        put.start()
        self.started.append(put)

    def arrived(self, dst, slot, device):
        self.copy(dst, dst, slot, device).wait_recv()

    def drain(self):
        for put in self.started:
            put.wait_send()


class Place:
    def __init__(self, groups, ranks):
        self.groups, self.ranks = groups, ranks
        self.t, self.s = lax.axis_index("teacher"), lax.axis_index("seq")
        self.core = self.t % 2
        self.bit = self.s % 2
        self.col = self.s // 2
        self.cols = ranks // 2
        self.sibling = {"teacher": self.t + 1 - 2 * self.core}
        self.across = {"teacher": (self.t + 2) % groups}
        self.partner = {"seq": self.s + 1 - 2 * self.bit}

    def later(self, step):
        return (self.s + step) % self.ranks

    def earlier(self, step):
        return (self.s + self.ranks - step) % self.ranks

    def barrier(self, seq=True, teacher=True):
        sem = pltpu.get_barrier_semaphore()
        count = 0
        if seq:
            for step in range(1, self.ranks):
                pl.semaphore_signal(
                    sem, inc=1, device_id={"seq": self.later(step)}, device_id_type=MESH
                )
                count += 1
        if teacher:
            for step in range(1, self.groups):
                pl.semaphore_signal(
                    sem,
                    inc=1,
                    device_id={"teacher": (self.t + step) % self.groups},
                    device_id_type=MESH,
                )
                count += 1
        pl.semaphore_wait(sem, count)


class Gather:
    def __init__(self, place, link, source, piece, chunks, spread=None):
        self.place, self.link, self.source, self.piece = place, link, source, piece
        self.chunks, self.spread = chunks, spread
        self.down = [link.take(place.cols) for _ in range(chunks)]
        self.over = [link.take(place.cols) for _ in range(chunks)]

    def shard(self, index):
        place = self.place
        bit = place.bit if index < place.cols else 1 - place.bit
        return ((place.col + place.cols - index % place.cols) % place.cols) * 2 + bit

    def start(self):
        place, link = self.place, self.link
        for chunk in range(self.chunks):
            source, target = self.source(chunk), self.piece(place.s, chunk)
            link.start(source, target, self.over[chunk], place.partner)
            for step in range(1, place.cols):
                peer = ((place.col + step) % place.cols) * 2 + place.bit
                link.start(source, target, self.down[chunk] + step, {"seq": peer})

    def forward(self, chunk):
        place, link = self.place, self.link
        for step in range(1, place.cols):
            shard = self.shard(step)
            ref = self.piece(shard, chunk)
            link.arrived(ref, self.down[chunk] + step, place.partner)
            link.start(ref, ref, self.over[chunk] + step, place.partner)
            if self.spread is not None:
                self.spread(shard, chunk, step)

    def collect(self, chunk):
        place, link = self.place, self.link
        for step in range(place.cols):
            shard = self.shard(place.cols + step)
            link.arrived(self.piece(shard, chunk), self.over[chunk] + step, place.partner)
            if self.spread is not None:
                self.spread(shard, chunk, place.cols + step)


def total_of(place, link, own, stage_t, stage_s):
    to_t, to_s = link.take(place.groups), link.take(place.ranks)

    def first():
        stage_t[place.t] = own[...]
        for step in range(1, place.groups):
            link.start(
                own,
                stage_t.at[place.t],
                to_t + step,
                {"teacher": (place.t + step) % place.groups},
            )

    def second():
        for step in range(1, place.groups):
            giver = (place.t + place.groups - step) % place.groups
            link.arrived(stage_t.at[giver], to_t + step, place.sibling)
        summed = stage_t[0]
        for group in range(1, place.groups):
            summed = summed + stage_t[group]
        stage_s[place.s] = summed
        for step in range(1, place.ranks):
            link.start(
                stage_s.at[place.s],
                stage_s.at[place.s],
                to_s + step,
                {"seq": place.later(step)},
            )

    def third():
        for step in range(1, place.ranks):
            link.arrived(stage_s.at[place.earlier(step)], to_s + step, place.partner)
        summed = stage_s[0]
        for rank in range(1, place.ranks):
            summed = summed + stage_s[rank]
        return summed

    return first, second, third


def columns(index, size):
    return pl.ds(pl.multiple_of(index * size, size), size)


def row_chunks(rows, most):
    return max(count for count in range(1, most + 1) if rows % (16 * count) == 0)


def projection_kernel(
    groups, ranks, proj, dilated, stats, full, dilated_all, totals,
    stage_t, stage_s, send, recv, local,
):
    place, link = Place(groups, ranks), Link(send, recv)
    chunks = row_chunks(proj.shape[0], 6)
    height = proj.shape[0] // chunks
    half = dilated.shape[2] // 2
    high = place.t // 2
    mine, other = columns(place.core, half), columns(1 - place.core, half)
    taps = (2 * high, 1, 2 - 2 * high)
    side, across = [link.take(ranks) for _ in taps], link.take(ranks)

    def to_sibling(shard, chunk, index):
        ref = dilated_all.at[taps[chunk], shard, :, mine]
        link.start(ref, ref, side[chunk] + index, place.sibling)

    def spread(shard, chunk, index):
        if chunk == 0:
            ref = dilated_all.at[taps[0], shard, :, mine]
            link.start(ref, ref, across + index, place.across)
        to_sibling(shard, chunk, index)

    place.barrier()
    keeps = [
        pltpu.make_async_copy(proj, full.at[place.s], local.at[0]),
        pltpu.make_async_copy(dilated, dilated_all.at[:, place.s], local.at[1]),
    ]
    for keep in keeps:
        keep.start()
    first, second, third = total_of(place, link, stats, stage_t, stage_s)
    gather = Gather(
        place,
        link,
        lambda q: proj.at[pl.ds(q * height, height)],
        lambda j, q: full.at[j, pl.ds(q * height, height)],
        chunks,
    )
    gather_d = Gather(
        place,
        link,
        lambda q: dilated.at[taps[q], :, mine],
        lambda j, q: dilated_all.at[taps[q], j, :, mine],
        2,
        spread,
    )
    first()
    gather_d.start()
    gather.start()
    second()
    for chunk in range(2):
        gather_d.forward(chunk)
        gather.forward(chunk)
    gather_d.collect(0)
    for chunk in range(2, chunks):
        gather.forward(chunk)
    gather_d.collect(1)
    for index in range(1, ranks):
        shard = gather_d.shard(index)
        link.arrived(dilated_all.at[taps[2], shard, :, mine], across + index, place.across)
        to_sibling(shard, 2, index)
    totals[...] = third()
    for chunk in range(chunks):
        gather.collect(chunk)
    for index in range(1, ranks):
        for chunk in range(3):
            ref = dilated_all.at[taps[chunk], gather_d.shard(index), :, other]
            link.arrived(ref, side[chunk] + index, place.sibling)
    for keep in keeps:
        keep.wait()
    link.drain()


def forward_kernel(
    groups, ranks, terms, pointwise, panels, hidden,
    terms_all, pointwise_all, panels_all, halo, send, recv, local,
):
    place, link = Place(groups, ranks), Link(send, recv)
    chunks = 2
    part = pointwise.shape[1] // (2 * chunks)
    bins = hidden.shape[1]
    place.barrier()
    to_t, to_s, edges = (link.take(count) for count in (groups, ranks, 2))
    side = [link.take(ranks) for _ in range(chunks)]
    after, before = {"seq": place.later(1)}, {"seq": place.earlier(1)}

    def part_of(core, chunk):
        return columns(core * chunks + chunk, part)

    def spread(shard, chunk, index):
        ref = pointwise_all.at[shard, :, part_of(place.core, chunk)]
        link.start(ref, ref, side[chunk] + index, place.sibling)

    for step in range(1, groups):
        taker = (place.t + step) % groups
        link.start(terms.at[taker], terms_all.at[place.t], to_t + step, {"teacher": taker})
    gather = Gather(
        place,
        link,
        lambda q: pointwise.at[:, part_of(place.core, q)],
        lambda j, q: pointwise_all.at[j, :, part_of(place.core, q)],
        chunks,
        spread,
    )
    gather.start()
    link.start(hidden.at[:, pl.ds(bins - TAP_DILATION, TAP_DILATION)], halo.at[0], edges, after)
    link.start(hidden.at[:, pl.ds(0, TAP_DILATION)], halo.at[1], edges + 1, before)
    for step in range(1, ranks):
        taker = place.later(step)
        link.start(panels.at[taker], panels_all.at[place.s], to_s + step, {"seq": taker})
    keeps = [
        pltpu.make_async_copy(terms.at[place.t], terms_all.at[place.t], local.at[0]),
        pltpu.make_async_copy(pointwise, pointwise_all.at[place.s], local.at[1]),
        pltpu.make_async_copy(panels.at[place.s], panels_all.at[place.s], local.at[2]),
    ]
    for keep in keeps:
        keep.start()
    for chunk in range(chunks):
        gather.forward(chunk)
    for chunk in range(chunks):
        gather.collect(chunk)
    for index in range(1, ranks):
        for chunk in range(chunks):
            ref = pointwise_all.at[gather.shard(index), :, part_of(1 - place.core, chunk)]
            link.arrived(ref, side[chunk] + index, place.sibling)
    link.arrived(halo.at[0], edges, after)
    link.arrived(halo.at[1], edges + 1, before)
    for step in range(1, groups):
        giver = (place.t + groups - step) % groups
        link.arrived(terms_all.at[giver], to_t + step, place.sibling)
    for step in range(1, ranks):
        link.arrived(panels_all.at[place.earlier(step)], to_s + step, place.partner)
    for keep in keeps:
        keep.wait()
    link.drain()


def backward_kernel(
    groups, ranks, slopes, partial, loss,
    slopes_all, from_chip, loss_total,
    from_core, stage_t, stage_s, send, recv, local,
):
    place, link = Place(groups, ranks), Link(send, recv)
    width = partial.shape[1] // groups
    rows = partial.shape[0] // ranks
    place.barrier()
    keep = pltpu.make_async_copy(slopes, slopes_all.at[place.s], local.at[0])
    keep.start()
    to_core, to_chip = link.take(1), link.take(1)
    high = place.t // 2

    link.start(partial.at[:, columns(1 - place.core, 2 * width)], from_core, to_core, place.sibling)
    first, second, third = total_of(place, link, loss, stage_t, stage_s)
    first()
    chunks = row_chunks(slopes.shape[0], 5)
    part = slopes.shape[0] // chunks
    gather = Gather(
        place,
        link,
        lambda q: slopes.at[pl.ds(q * part, part)],
        lambda j, q: slopes_all.at[j, pl.ds(q * part, part)],
        chunks,
    )
    gather.start()
    link.arrived(from_core, to_core, place.sibling)
    mine = columns(place.core, 2 * width)

    @pl.loop(0, ranks)
    def _(rank):
        span = pl.ds(pl.multiple_of(rank * rows, rows), rows)
        from_core[span] = from_core[span] + partial[span, mine]

    link.start(from_core.at[:, columns(1 - high, width)], from_chip, to_chip, place.across)
    gather.forward(0)
    second()
    gather.forward(1)
    link.arrived(from_chip, to_chip, place.across)
    kept = columns(high, width)

    @pl.loop(0, ranks)
    def _(rank):
        span = pl.ds(pl.multiple_of(rank * rows, rows), rows)
        from_chip[span] = from_chip[span] + from_core[span, kept]

    for chunk in range(2, chunks):
        gather.forward(chunk)
    for chunk in range(chunks):
        gather.collect(chunk)
    loss_total[...] = third()
    keep.wait()
    link.drain()


def share_kernel(
    groups, ranks, partial, block, out, shares, from_core, from_chip, pieces, send, recv
):
    place, link = Place(groups, ranks), Link(send, recv)
    taps, depth, branch = partial.shape
    half, tall = branch // 2, depth // 2
    rows, width = block.shape[0] // ranks, block.shape[1]
    parts = [(tap, pl.ds(low, tall)) for tap in range(taps) for low in (0, tall)]
    a, b, c = (link.take(len(parts)) for _ in range(3))
    to_s, to_t = link.take(ranks), link.take(groups)
    mine, other = columns(place.core, half), columns(1 - place.core, half)
    place.barrier()
    for at, (tap, span) in enumerate(parts):
        link.start(
            partial.at[tap, span, other], from_core.at[tap, span], a + at, place.sibling
        )
    for step in range(1, ranks):
        taker = place.later(step)
        span = pl.ds(pl.multiple_of(taker * rows, rows), rows)
        link.start(block.at[span], pieces.at[place.s], to_s + step, {"seq": taker})
    for at, (tap, span) in enumerate(parts):
        link.arrived(from_core.at[tap, span], a + at, place.sibling)
        from_core[tap, span] = from_core[tap, span] + partial[tap, span, mine]
        link.start(from_core.at[tap, span], from_chip.at[tap, span], b + at, place.across)
    pieces[place.s] = block[pl.ds(pl.multiple_of(place.s * rows, rows), rows)]

    def add_chip(at):
        tap, span = parts[at]
        link.arrived(from_chip.at[tap, span], b + at, place.across)
        out[tap, span, mine] = from_chip[tap, span] + from_core[tap, span]
        link.start(out.at[tap, span, mine], out.at[tap, span, mine], c + at, place.sibling)

    for at in range(len(parts) - 1):
        add_chip(at)
    for step in range(1, ranks):
        link.arrived(pieces.at[place.earlier(step)], to_s + step, place.partner)
    summed = pieces[0]
    for rank in range(1, ranks):
        summed = summed + pieces[rank]
    kept = columns(place.core * 2 + place.t // 2, width)
    shares[:, kept] = summed
    for step in range(1, groups):
        link.start(
            shares.at[:, kept],
            shares.at[:, kept],
            to_t + step,
            {"teacher": (place.t + step) % groups},
        )
    add_chip(len(parts) - 1)
    for at, (tap, span) in enumerate(parts):
        link.arrived(out.at[tap, span, other], c + at, place.sibling)
    for step in range(1, groups):
        giver = (place.t + groups - step) % groups
        ref = shares.at[:, columns((giver % 2) * 2 + giver // 2, width)]
        link.arrived(ref, to_t + step, place.sibling)
    link.drain()


def exchange(kernel, number, groups, ranks, args, specs, outs, out_specs, scratch, copies, locals_):
    sems = [pltpu.SemaphoreType.DMA((copies,)), pltpu.SemaphoreType.DMA((copies,))]
    if locals_:
        sems.append(pltpu.SemaphoreType.DMA((locals_,)))
    return pl.pallas_call(
        functools.partial(kernel, groups, ranks),
        out_shape=[jax.ShapeDtypeStruct(shape, kind) for shape, kind in outs],
        in_specs=specs,
        out_specs=out_specs,
        scratch_shapes=[pltpu.VMEM(shape, kind) for shape, kind in scratch] + sems,
        compiler_params=pltpu.CompilerParams(
            collective_id=number, has_side_effects=True, vmem_limit_bytes=40 * 1024 * 1024
        ),
    )(*args)


def gelu_tanh(value):
    inside = slope_const * (value + cubic_const * value * value * value)
    return 0.5 * value * (1.0 + jnp.tanh(inside))


def gelu_slope(value):
    inside = slope_const * (value + cubic_const * value * value * value)
    tangent = jnp.tanh(inside)
    return 0.5 * (1.0 + tangent) + 0.5 * value * (1.0 - tangent * tangent) * slope_const * (
        1.0 + 3.0 * cubic_const * value * value
    )


def column_product(left, right):
    return lax.dot_general(
        left, right, (((0,), (0,)), ((), ())), preferred_element_type=jnp.float32
    )


def shards(activations, teacher_maps, projection, dilated_weight, pointwise_weight):
    groups = lax.axis_size("teacher")
    ranks = lax.axis_size("seq")
    f32, bf16 = jnp.float32, jnp.bfloat16
    win_grp, bins, channels = activations.shape
    branch = dilated_weight.shape[2]
    panel = dilated_weight.shape[0]
    features = projection.shape[1]
    rows = win_grp * bins
    total_rows = rows * groups * ranks
    rank = lax.axis_index("seq")

    inputs_f = activations.reshape(rows, channels).astype(f32)
    stats = jnp.concatenate(
        [
            jnp.sum(inputs_f, axis=0, keepdims=True),
            jnp.sum(inputs_f * inputs_f, axis=0, keepdims=True),
            jnp.zeros((6, channels), f32),
        ]
    )
    proj_full, dilated_all, totals = exchange(
        projection_kernel, 0, groups, ranks,
        (projection[0], dilated_weight.transpose(1, 0, 2), stats), [HBM, HBM, VMEM],
        [
            ((ranks, features, channels), bf16),
            ((3, ranks, panel, branch), bf16),
            ((8, channels), f32),
        ],
        [HBM, HBM, VMEM],
        [((groups, 8, channels), f32), ((ranks, 8, channels), f32)],
        13 * ranks + groups, 2,
    )
    channel_mean = totals[0] / total_rows
    channel_var = totals[1] / total_rows - channel_mean * channel_mean
    normed = (inputs_f - channel_mean) * lax.rsqrt(channel_var + 1e-05)
    hidden = gelu_tanh(normed).astype(bf16)
    hidden_3d = hidden.reshape(win_grp, bins, channels)
    panels = jnp.stack([hidden[:, j * panel : (j + 1) * panel] for j in range(ranks)])
    terms = jnp.dot(
        teacher_maps[0].reshape(groups * rows, -1),
        proj_full.reshape(ranks * features, channels),
        preferred_element_type=f32,
    ).astype(bf16)

    terms_all, pointwise_all, panels_all, halo = exchange(
        forward_kernel, 1, groups, ranks,
        (
            terms.reshape(groups, rows, channels),
            pointwise_weight,
            panels,
            hidden_3d,
        ),
        [HBM] * 4,
        [
            ((groups, rows, channels), bf16),
            ((ranks,) + pointwise_weight.shape, bf16),
            ((ranks, rows, panel), bf16),
            ((2, win_grp, TAP_DILATION, channels), bf16),
        ],
        [HBM] * 4,
        [],
        5 * ranks + groups + 2, 3,
    )
    target = terms_all[0].astype(f32)
    for group in range(1, groups):
        target = target + terms_all[group].astype(f32)
    target = target / groups

    low = jnp.where(rank > 0, halo[0], jnp.zeros_like(halo[0]))
    high = jnp.where(rank < ranks - 1, halo[1], jnp.zeros_like(halo[1]))
    padded = jnp.concatenate([low, hidden_3d, high], axis=1)
    shifted = jnp.concatenate(
        [padded[:, tap * TAP_DILATION : tap * TAP_DILATION + bins] for tap in range(3)], axis=2
    )
    preact = jnp.dot(
        shifted.reshape(rows, 3 * channels),
        dilated_all.reshape(3 * channels, branch),
        preferred_element_type=f32,
    )
    activated = gelu_tanh(preact).astype(bf16)
    pointwise_full = pointwise_all.reshape(branch, channels)
    student = inputs_f + jnp.dot(activated, pointwise_full, preferred_element_type=f32)
    misfit = student - target
    squared = jnp.sum(misfit * misfit)
    out_grad = (misfit / channels).astype(bf16)
    back_grad = lax.dot_general(
        out_grad, pointwise_full, (((1,), (1,)), ((), ())), preferred_element_type=f32
    )
    preact_grad = (back_grad * gelu_slope(preact)).astype(bf16)
    pointwise_part = column_product(activated, out_grad)

    slopes_all, block, loss_total = exchange(
        backward_kernel, 2, groups, ranks,
        (preact_grad, pointwise_part, jnp.full((8, 128), squared, f32)),
        [HBM, VMEM, VMEM],
        [
            ((ranks, rows, branch), bf16),
            ((branch, channels // groups), f32),
            ((8, 128), f32),
        ],
        [HBM, VMEM, VMEM],
        [
            ((branch, channels // 2), f32),
            ((groups, 8, 128), f32),
            ((ranks, 8, 128), f32),
        ],
        6 * ranks + groups + 2, 1,
    )
    loss_mean = 0.5 * loss_total[0, 0] / (channels * total_rows)

    def windows(blocks):
        return (
            blocks.reshape(ranks, win_grp, bins, -1)
            .transpose(1, 0, 2, 3)
            .reshape(win_grp, ranks * bins, -1)
        )

    hidden_w = jnp.pad(windows(panels_all), ((0, 0), (TAP_DILATION, TAP_DILATION), (0, 0)))
    slopes_w = windows(slopes_all).reshape(win_grp * ranks * bins, branch)
    partial = jnp.stack(
        [
            column_product(
                hidden_w[:, tap * TAP_DILATION : tap * TAP_DILATION + ranks * bins].reshape(
                    win_grp * ranks * bins, panel
                ),
                slopes_w,
            )
            for tap in range(3)
        ]
    )
    dilated_grad, pointwise_grad = exchange(
        share_kernel, 3, groups, ranks,
        (partial, block), [VMEM, VMEM],
        [((3, panel, branch), f32), ((branch // ranks, channels), f32)], [VMEM, VMEM],
        [
            ((3, panel, branch // 2), f32),
            ((3, panel, branch // 2), f32),
            ((ranks, branch // ranks, channels // groups), f32),
        ],
        18 + ranks + groups, 0,
    )
    return (loss_mean, dilated_grad.transpose(1, 0, 2), pointwise_grad)


def solution(mesh):
    in_specs = (
        P("teacher", "seq", None),
        P("teacher", None, "seq", None),
        P("teacher", "seq", None),
        P("seq", None, None),
        P("seq", None),
    )
    out_specs = (P(), P("seq", None, None), P("seq", None))
    return jax.shard_map(shards, mesh=mesh, in_specs=in_specs, out_specs=out_specs, check_vma=False)
```
